256 devices in a mesh: dp: 32 (over z_hi, x, core), tensor: 8 (over y, z_lo).
Axes of the slice: x: 4, y: 4, z: 8 (z_hi: 4, z_lo: 2; z = z_hi * 2 + z_lo), core: 2. Of those that a mesh axis runs over, the one named last changes fastest.
Arguments:
- queries: bfloat16 [8192, 7680], P('dp', 'tensor'), may hold values from -16 to 16
- keys_values: bfloat16 [8192, 1024], P('dp', 'tensor'), may hold values from -16 to 16
- out_weight: bfloat16 [7424, 7680], P('dp', 'tensor'), may hold values from -0.0625 to 0.0625
- cotangent: bfloat16 [8192, 7424], P('dp', 'tensor'), may hold values from -6 to 6
Outputs:
- block_out: bfloat16 [8192, 7424], P('dp', 'tensor')
- grad_queries: bfloat16 [8192, 7680], P('dp', 'tensor')
- grad_keys_values: bfloat16 [8192, 1024], P('dp', 'tensor')
- grad_out_weight: bfloat16 [7424, 7680], P('dp', 'tensor')
The draws below stay inside these ranges and needn't reach their ends.
All inputs are finite; a program needn't handle non-finite values.
Results may differ from the reference program's by a relative error of at most 0.024.
Values may be sent and summed in bfloat16 or wider, within the bound.
A program may use at most 128 MiB of HBM per device.

```python
import math
import jax
import jax.numpy as jnp
from jax import lax

D = 7424
QH = 120
KVH = 8
HD = 64
TOK_DEV = 256
TOKENS = 8192
N_TENSOR = 8


def paired_fields(key, align_gain):
    split_keys = [jax.random.fold_in(key, c) for c in (21, 22, 23, 24)]
    query_shape = (TOKENS, QH, HD)
    pair_shape = (TOKENS, KVH, 2, HD)
    query_normal = jnp.clip(jax.random.normal(split_keys[0], query_shape, jnp.float32), -4.0, 4.0)
    query_base = query_normal
    pair_normal = jnp.clip(jax.random.normal(split_keys[2], pair_shape, jnp.float32), -4.0, 4.0)
    pair_base = pair_normal
    position = jnp.arange(TOKENS) % TOK_DEV
    slot_phase = position % 16
    drawn_keys = pair_base[:, :, 0, :]
    scaled_keys = drawn_keys
    pairs_out = jnp.stack([scaled_keys, pair_base[:, :, 1, :]], axis=2)
    select = (slot_phase == 15).astype(jnp.float32) * align_gain
    queries_out = (1.0 - select[:, None, None]) * query_base
    return (queries_out.reshape(TOKENS, QH * HD), pairs_out.reshape(TOKENS, 2 * KVH * HD))


def draw_queries(key, part):
    fields = paired_fields(key, 0.0)
    return fields[0].astype(jnp.bfloat16)


def draw_keys_values(key, part):
    fields = paired_fields(key, 0.0)
    return fields[1].astype(jnp.bfloat16)


def spiked(drawn, key, source, target, shards_of, factor):
    owner, partner = [(jnp.arange(drawn.shape[axis_at]) // (drawn.shape[axis_at] // shards_of)).reshape([-1 if axis == axis_at else 1 for axis in range(drawn.ndim)]) for axis_at in (source, target)]
    chosen = jax.random.permutation(key, shards_of)[partner]
    strong = (owner == chosen) | (owner == (partner + shards_of // 2) % shards_of)
    return jnp.where(strong, factor * drawn, drawn)


def level_of(own_key, extent, shards, least, largest):
    def one(axis_at, shards_of):
        heights = jax.random.uniform(jax.random.fold_in(jax.random.fold_in(own_key, 6), axis_at), (shards_of,), jnp.float32, least / len(shards), largest / len(shards))
        return jnp.repeat(jnp.exp(heights), extent[axis_at] // shards_of).reshape((-1,) + (1,) * (len(extent) - axis_at - 1))

    gain = one(*shards[0])
    for cut in shards[1:]:
        gain = gain * one(*cut)
    return gain


def normal_values(rng, shape, spread, reach, cuts=(), held_as=jnp.bfloat16):
    array = spread * jax.random.normal(rng, shape, jnp.float32)
    if cuts:
        array = array * level_of(rng, shape, cuts, -0.22, 0.18)
    return jnp.clip(array, -reach, reach).astype(held_as)


def heavy_noise(stream_key, shape, width, limit, split, heavy, dtype=jnp.bfloat16):
    result = width * jax.random.normal(stream_key, shape, jnp.float32)
    if split:
        result = result * level_of(stream_key, shape, split, -0.22, 0.18)
    return jnp.clip(spiked(result, jax.random.fold_in(stream_key, 3), *heavy), -limit, limit).astype(dtype)


def setup_inputs(seed: int = 0) -> dict:
    keys = jax.random.split(jax.random.key(seed), 5)
    queries = draw_queries(jax.random.fold_in(keys[4], 71), 0)
    keys_values = draw_keys_values(jax.random.fold_in(keys[4], 71), 0)
    out_weight = normal_values(keys[2], (D, QH * HD), (QH * HD) ** -0.5, 0.0625, ((0, 32), (1, 8)))
    cotangent = heavy_noise(keys[3], (TOKENS, D), 1.0, 6.0, ((0, 32), (1, 8)), (0, 1, 32, 2.75))
    return dict(queries=queries, keys_values=keys_values, out_weight=out_weight, cotangent=cotangent)


masked_score = -1e+30

def rounded(values):
    return lax.optimization_barrier(values.astype(jnp.bfloat16)).astype(jnp.float32)

def attend_one(q_seq, kv_seq, grad_seq):
    length = q_seq.shape[0]
    scaling = 1.0 / math.sqrt(HD)
    groups = QH // KVH
    q_heads = q_seq.astype(jnp.float32).reshape(length, KVH, groups, HD)
    kv_pairs = kv_seq.astype(jnp.float32).reshape(length, KVH, 2, HD)
    key_rows = kv_pairs[:, :, 0]
    value_rows = kv_pairs[:, :, 1]
    scores = jnp.einsum('ikgd,jkd->kgij', q_heads, key_rows) * scaling
    causal = jnp.arange(length)[:, None] >= jnp.arange(length)[None, :]
    scores = jnp.where(causal, scores, masked_score)
    lifted = jnp.exp(scores - lax.optimization_barrier(jnp.max(scores, axis=-1, keepdims=True)))
    softmax_p = lifted / lax.optimization_barrier(jnp.sum(lifted, axis=-1, keepdims=True))
    weights = rounded(softmax_p)
    attended = jnp.einsum('kgij,jkd->ikgd', weights, value_rows).astype(jnp.bfloat16).reshape(length, QH * HD)
    grad_heads = grad_seq.astype(jnp.float32).reshape(length, KVH, groups, HD)
    grad_p = jnp.einsum('ikgd,jkd->kgij', grad_heads, value_rows)
    row_dot = lax.optimization_barrier(jnp.sum(softmax_p * grad_p, axis=-1, keepdims=True))
    grad_scores = rounded(softmax_p * (grad_p - row_dot) * scaling)
    grad_q = jnp.einsum('kgij,jkd->ikgd', grad_scores, key_rows).astype(jnp.bfloat16).reshape(length, QH * HD)
    grad_k = jnp.einsum('kgij,ikgd->jkd', grad_scores, q_heads)
    grad_v = jnp.einsum('kgij,ikgd->jkd', weights, grad_heads)
    grad_kv = jnp.stack([grad_k, grad_v], axis=2).astype(jnp.bfloat16).reshape(length, 2 * KVH * HD)
    return (attended, grad_q, grad_kv)

def reference(queries, keys_values, out_weight, cotangent):
    sequences = TOKENS // TOK_DEV
    grad_attn = jnp.dot(cotangent, out_weight, preferred_element_type=jnp.float32).astype(jnp.bfloat16)

    def per_sequence(inputs):
        return attend_one(inputs[0], inputs[1], inputs[2])
    attended, grad_q, grad_kv = lax.map(per_sequence, (queries.reshape(sequences, TOK_DEV, QH * HD), keys_values.reshape(sequences, TOK_DEV, 2 * KVH * HD), grad_attn.reshape(sequences, TOK_DEV, QH * HD)))
    attended = attended.reshape(TOKENS, QH * HD)
    grad_q = grad_q.reshape(TOKENS, QH * HD)
    grad_kv = grad_kv.reshape(TOKENS, 2 * KVH * HD)
    head_cols = QH * HD // N_TENSOR
    summed = jnp.zeros((TOKENS, D), jnp.float32)
    for block in range(N_TENSOR):
        first_col = block * head_cols
        partial_value = jnp.dot(attended[:, first_col:first_col + head_cols], out_weight[:, first_col:first_col + head_cols].T, preferred_element_type=jnp.float32)
        summed = summed + rounded(partial_value)
    block_out = summed.astype(jnp.bfloat16)

    def accumulate(running, inputs):
        partial_value = jnp.dot(inputs[0].T, inputs[1], preferred_element_type=jnp.float32) * (1.0 / TOK_DEV)
        return (running + rounded(partial_value), None)
    grad_weight, unused = lax.scan(accumulate, jnp.zeros((D, QH * HD), jnp.float32), (cotangent.reshape(sequences, TOK_DEV, D), attended.reshape(sequences, TOK_DEV, QH * HD)))
    return (block_out, grad_q, grad_kv, grad_weight.astype(jnp.bfloat16))
```

```python
import functools
import math

import jax
import jax.numpy as jnp
from jax import lax
from jax.experimental import pallas as pl
from jax.experimental.pallas import tpu as pltpu
from jax.sharding import PartitionSpec as P

MESH = pl.DeviceIdType.MESH
HD = 64
HEADS = 15
TOK = 256
HCOL = HEADS * HD
ROWS = 232
PAD = 240
SEGMENT = 5
MASKED = -1e30
BF = jnp.bfloat16
F32 = jnp.float32


def device(zh, x, c, y, zl):
    return (zh * 8 + x * 2 + c, y * 2 + zl)


def kernel(
    q_t, kv, kv_t, w_in, cot_in,
    out_o, gq_o, gkv_o, gw_o,
    cz, cot_all, w_all, att_all, probs, w_t,
    o_part, o_recv, rx, rz, g_part, g_core, g_recv, a_part, a_recv, gkv_acc,
    zl_s, zl_r, xa_s, xa_r, yg_s, yg_r, zg_s, zg_r, wc_s, wc_r, xg_s, xg_r,
    yr_s, yr_r, xo_s, xo_r, zo_s, zo_r, gc_s, gc_r, zr_s, zr_r, ar_s, ar_r,
):
    dp = lax.axis_index("dp")
    tensor = lax.axis_index("tensor")
    zh, x, c = dp // 8, (dp // 2) % 4, dp % 2
    y, zl = tensor // 2, tensor % 2
    sign = 1 - 2 * c
    x_p, x_m, x_2 = (x + 4 + sign) % 4, (x + 4 - sign) % 4, (x + 2) % 4
    y_p, y_m, y_2 = (y + 4 + sign) % 4, (y + 4 - sign) % 4, (y + 2) % 4
    z_p, z_m, z_2 = (zh + 4 + sign) % 4, (zh + 4 - sign) % 4, (zh + 2) % 4
    at_x = lambda other: device(zh, other, c, y, zl)
    at_y = lambda other: device(zh, x, c, other, zl)
    at_z = lambda other: device(other, x, c, y, zl)
    sibling = device(zh, x, 1 - c, y, zl)
    partner = device(zh, x, c, y, 1 - zl)

    def send(src, dst, send_sem, recv_sem, to):
        return pltpu.make_async_remote_copy(
            src_ref=src, dst_ref=dst, send_sem=send_sem, recv_sem=recv_sem,
            device_id=to, device_id_type=MESH,
        )

    started = []

    def start(*args):
        copy = send(*args)
        copy.start()
        started.append(copy)
        return copy

    barrier = pltpu.get_barrier_semaphore()
    others = [sibling, partner, at_x(x_p), at_x(x_m), at_x(x_2)]
    others += [at_y(y_p), at_y(y_m), at_z(z_p), at_z(z_m)]
    for other in others:
        pl.semaphore_signal(barrier, inc=1, device_id=other, device_id_type=MESH)
    pl.semaphore_wait(barrier, len(others))

    zl_copy = start(cot_in, cz.at[zl], zl_s.at[0], zl_r.at[0], partner)
    cz[zl] = cot_in[...]
    w_all[zh, c] = w_in[...]

    row = lax.broadcasted_iota(jnp.int32, (TOK, TOK), 0)
    col = lax.broadcasted_iota(jnp.int32, (TOK, TOK), 1)
    allowed = row <= col
    scale = 1.0 / math.sqrt(HD)

    def forward_head(h, carry):
        rows = pl.ds(pl.multiple_of(h * HD, HD), HD)
        scores = jnp.dot(kv[:, :HD], q_t[rows, :], preferred_element_type=F32)
        scores = jnp.where(allowed, scores * scale, MASKED)
        lifted = jnp.exp(scores - jnp.max(scores, axis=0, keepdims=True))
        soft = lifted / jnp.sum(lifted, axis=0, keepdims=True)
        probs[h] = soft
        attended = jnp.dot(kv_t[HD:, :], soft.astype(BF), preferred_element_type=F32)
        att_all[x, rows, :] = attended.astype(BF)
        return carry

    att_copies = []

    def attention_segment(k):
        lax.fori_loop(k * SEGMENT, (k + 1) * SEGMENT, forward_head, 0)
        part = att_all.at[x, pl.ds(k * SEGMENT * HD, SEGMENT * HD)]
        first = start(part, part, xg_s.at[0, k], xg_r.at[0, k], at_x(x_p))
        second = start(part, part, xg_s.at[1, k], xg_r.at[1, k], at_x(x_m))
        att_copies.append((first, second))

    attention_segment(0)
    attention_segment(1)

    zl_copy.wait_recv()
    w_p = start(w_in, w_all.at[zh, c], zg_s.at[0], zg_r.at[0], at_z(z_p))
    w_m = start(w_in, w_all.at[zh, c], zg_s.at[1], zg_r.at[1], at_z(z_m))
    w_c = [start(w_in, w_all.at[zh, c], wc_s.at[0], wc_r.at[0], sibling)]
    xa = []
    for d in (1, 2, 3):
        to = (x + d) % 4
        piece = cz.at[to // 2, pl.ds(2 * (to % 2), 2)]
        xa.append(start(piece, cot_all.at[y, x], xa_s.at[d - 1], xa_r.at[d - 1], at_x(to)))
    cot_all[y, x] = cz[x // 2, pl.ds(2 * (x % 2), 2)]

    attention_segment(2)

    yg = []

    def y_start(k, j):
        block = cot_all.at[y, j]
        first = start(block, block, yg_s.at[0, k], yg_r.at[0, k], at_y(y_p))
        second = start(block, block, yg_s.at[1, k], yg_r.at[1, k], at_y(y_m))
        yg.append((first, second))

    y_start(0, x)
    for k in (1, 3, 2):
        xa[k - 1].wait_recv()
        y_start(k, (x + 4 - k) % 4)

    forwarded = []
    for k in range(3):
        att_copies[k][0].wait_recv()
        part = att_all.at[x_m, pl.ds(k * SEGMENT * HD, SEGMENT * HD)]
        forwarded.append(start(part, part, xg_s.at[2, k], xg_r.at[2, k], at_x(x_p)))

    w_p.wait_recv()
    block = w_all.at[z_m, c]
    w_f = start(block, block, zg_s.at[2], zg_r.at[2], at_z(z_p))
    w_c.append(start(block, block, wc_s.at[1], wc_r.at[1], sibling))
    w_m.wait_recv()
    block = w_all.at[z_p, c]
    w_c.append(start(block, block, wc_s.at[2], wc_r.at[2], sibling))

    yf = []
    for i, k in enumerate((0, 1, 3, 2)):
        yg[i][0].wait_recv()
        block = cot_all.at[y_m, (x + 4 - k) % 4]
        yf.append(start(block, block, yg_s.at[2, k], yg_r.at[2, k], at_y(y_p)))

    for k in range(3):
        att_copies[k][1].wait_recv()
        forwarded[k].wait_recv()
    w_f.wait_recv()
    block = w_all.at[z_2, c]
    w_c.append(start(block, block, wc_s.at[3], wc_r.at[3], sibling))
    for copy in w_c:
        copy.wait_recv()

    def out_partial(dest):
        weight = w_all[dest].reshape(2 * PAD, HCOL)

        def one(j, carry):
            value = jnp.dot(weight, att_all[j], preferred_element_type=F32)
            o_part[dest, j] = value.astype(BF).reshape(2, PAD, TOK)
            return carry

        lax.fori_loop(0, 4, one, 0)

    out_partial(y_2)
    yr0 = [start(o_part.at[y_2, j], o_recv.at[0, j], yr_s.at[0, j], yr_r.at[0, j], at_y(y_m)) for j in range(4)]
    out_partial(y_p)
    yr1 = [start(o_part.at[y_p, j], o_recv.at[1, j], yr_s.at[1, j], yr_r.at[1, j], at_y(y_p)) for j in range(4)]
    out_partial(y_m)
    out_partial(y)

    def transpose_weight(k, carry):
        w_t[k] = jnp.transpose(w_all[k].reshape(2 * PAD, HCOL))
        return carry

    lax.fori_loop(0, 4, transpose_weight, 0)

    for i in range(4):
        yg[i][1].wait_recv()
        yf[i].wait_recv()

    def weight_partial(dest):
        total = jnp.zeros((2 * PAD, HCOL), F32)
        for j in range(4):
            total += lax.dot_general(
                cot_all[dest, j].reshape(2 * PAD, TOK), att_all[j],
                (((1,), (1,)), ((), ())), preferred_element_type=F32,
            )
        g_part[dest] = (total * (1.0 / TOK)).astype(BF).reshape(2, PAD, HCOL)

    gc = []

    def weight_step(k, dest):
        weight_partial(dest)
        gc.append(start(g_part.at[dest, 1 - c], g_core.at[dest], gc_s.at[dest], gc_r.at[dest], sibling))

    def attended_partial(dest):
        total = jnp.zeros((HCOL, TOK), F32)
        for k in range(4):
            total += jnp.dot(w_t[k], cot_all[k, dest].reshape(2 * PAD, TOK), preferred_element_type=F32)
        a_part[dest] = total.astype(BF)

    def add_out(dest, kind, j):
        value = o_part[dest, j].astype(F32) + o_recv[kind, j].astype(F32)
        o_part[dest, j] = value.astype(BF)

    attended_partial(x_2)
    ar0 = start(a_part.at[x_2], a_recv.at[0], ar_s.at[0], ar_r.at[0], at_x(x_m))
    weight_step(0, z_2)
    yr2 = []
    for j in range(4):
        yr0[j].wait_recv()
        add_out(y_m, 0, j)
        yr2.append(start(o_part.at[y_m, j], o_recv.at[2, j], yr_s.at[2, j], yr_r.at[2, j], at_y(y_m)))
    attended_partial(x_p)
    ar1 = start(a_part.at[x_p], a_recv.at[1], ar_s.at[1], ar_r.at[1], at_x(x_p))
    attended_partial(x_m)
    ar0.wait_recv()
    a_part[x_m] = (a_part[x_m].astype(F32) + a_recv[0].astype(F32)).astype(BF)
    ar2 = start(a_part.at[x_m], a_recv.at[2], ar_s.at[2], ar_r.at[2], at_x(x_m))

    def weight_join(k, dest):
        gc[k].wait_recv()
        g_part[dest, c] = (g_part[dest, c].astype(F32) + g_core[dest].astype(F32)).astype(BF)

    weight_join(0, z_2)
    zr0 = start(g_part.at[z_2, c], g_recv.at[0], zr_s.at[0], zr_r.at[0], at_z(z_m))
    weight_step(1, z_p)
    weight_step(2, z_m)
    weight_join(1, z_p)
    zr1 = start(g_part.at[z_p, c], g_recv.at[1], zr_s.at[1], zr_r.at[1], at_z(z_p))
    weight_step(3, zh)
    attended_partial(x)
    weight_join(2, z_m)
    zr0.wait_recv()
    g_part[z_m, c] = (g_part[z_m, c].astype(F32) + g_recv[0].astype(F32)).astype(BF)
    zr2 = start(g_part.at[z_m, c], g_recv.at[2], zr_s.at[2], zr_r.at[2], at_z(z_m))

    ar1.wait_recv()
    ar2.wait_recv()
    a_part[x] = (
        a_part[x].astype(F32) + a_recv[1].astype(F32) + a_recv[2].astype(F32)
    ).astype(BF)

    gkv_acc[...] = jnp.zeros_like(gkv_acc)

    def backward_head(h, carry):
        rows = pl.ds(pl.multiple_of(h * HD, HD), HD)
        grad = a_part[x, rows, :]
        soft = probs[h]
        grad_p = jnp.dot(kv[:, HD:], grad, preferred_element_type=F32)
        dot = jnp.sum(soft * grad_p, axis=0, keepdims=True)
        grad_s = (soft * (grad_p - dot) * scale).astype(BF)
        gq_o[rows, :] = jnp.dot(kv_t[:HD, :], grad_s, preferred_element_type=F32).astype(BF)
        last = (((1,), (1,)), ((), ()))
        gkv_acc[:HD, :] += lax.dot_general(q_t[rows, :], grad_s, last, preferred_element_type=F32)
        gkv_acc[HD:, :] += lax.dot_general(grad, soft.astype(BF), last, preferred_element_type=F32)
        return carry

    lax.fori_loop(0, 8, backward_head, 0)

    def out_final(j):
        value = o_part[y, j].astype(F32) + o_recv[1, j].astype(F32) + o_recv[2, j].astype(F32)
        return value.astype(BF)

    for j in range(4):
        yr1[j].wait_recv()
        yr2[j].wait_recv()
    xo = []
    for d in (2, 1, 3):
        to = (x + d) % 4
        o_part[y, to] = out_final(to)
        xo.append(start(o_part.at[y, to], rx.at[x], xo_s.at[d - 1], xo_r.at[d - 1], at_x(to)))
    rx[x] = out_final(x)

    lax.fori_loop(8, HEADS, backward_head, 0)
    gkv_o[...] = gkv_acc[...].astype(BF)

    for copy in xo:
        copy.wait_recv()
    zo = start(rx.at[pl.ds(2 * (1 - zl), 2)], rz, zo_s.at[0], zo_r.at[0], partner)

    weight_join(3, zh)
    zr1.wait_recv()
    zr2.wait_recv()
    gw_o[...] = (
        g_part[zh, c].astype(F32) + g_recv[1].astype(F32) + g_recv[2].astype(F32)
    ).astype(BF)

    zo.wait_recv()
    for h in range(2):
        value = rx[2 * zl + h].astype(F32) + rz[h].astype(F32)
        out_o[pl.ds(2 * h, 2)] = value.astype(BF)
    for copy in started:
        copy.wait_send()


def body(queries, keys_values, out_weight, cotangent):
    q_t = queries.T
    kv_t = keys_values.T
    w_in = jnp.pad(out_weight, ((0, PAD - ROWS), (0, 0)))
    cot = jnp.pad(cotangent.T.reshape(4, ROWS, TOK), ((0, 0), (0, PAD - ROWS), (0, 0)))
    vmem = pl.BlockSpec(memory_space=pltpu.VMEM)
    dma = lambda *shape: pltpu.SemaphoreType.DMA(shape)
    scratch = [
        pltpu.VMEM((2, 4, PAD, TOK), BF),
        pltpu.VMEM((4, 4, 2, PAD, TOK), BF),
        pltpu.VMEM((4, 2, PAD, HCOL), BF),
        pltpu.VMEM((4, HCOL, TOK), BF),
        pltpu.VMEM((HEADS, TOK, TOK), F32),
        pltpu.VMEM((4, HCOL, 2 * PAD), BF),
        pltpu.VMEM((4, 4, 2, PAD, TOK), BF),
        pltpu.VMEM((3, 4, 2, PAD, TOK), BF),
        pltpu.VMEM((4, 2, PAD, TOK), BF),
        pltpu.VMEM((2, 2, PAD, TOK), BF),
        pltpu.VMEM((4, 2, PAD, HCOL), BF),
        pltpu.VMEM((4, PAD, HCOL), BF),
        pltpu.VMEM((3, PAD, HCOL), BF),
        pltpu.VMEM((4, HCOL, TOK), BF),
        pltpu.VMEM((3, HCOL, TOK), BF),
        pltpu.VMEM((2 * HD, TOK), F32),
        dma(1), dma(1), dma(3), dma(3), dma(3, 4), dma(3, 4), dma(3), dma(3), dma(4), dma(4),
        dma(3, 3), dma(3, 3), dma(3, 4), dma(3, 4), dma(3), dma(3), dma(1), dma(1),
        dma(4), dma(4), dma(3), dma(3), dma(3), dma(3),
    ]
    out, gq, gkv, gw = pl.pallas_call(
        kernel,
        out_shape=(
            jax.ShapeDtypeStruct((4, PAD, TOK), BF),
            jax.ShapeDtypeStruct((HCOL, TOK), BF),
            jax.ShapeDtypeStruct((2 * HD, TOK), BF),
            jax.ShapeDtypeStruct((PAD, HCOL), BF),
        ),
        in_specs=[vmem] * 5,
        out_specs=(vmem,) * 4,
        scratch_shapes=scratch,
        compiler_params=pltpu.CompilerParams(
            collective_id=0, has_side_effects=True, vmem_limit_bytes=60 * 2**20
        ),
        cost_estimate=pl.CostEstimate(flops=12 * 10**9, bytes_accessed=5 * 10**6, transcendentals=10**6),
    )(q_t, keys_values, kv_t, w_in, cot)
    block_out = out[:, :ROWS].reshape(4 * ROWS, TOK).T
    return block_out, gq.T, gkv.T, gw[:ROWS]


def solution(mesh):
    spec = P("dp", "tensor")
    return jax.shard_map(
        body, mesh=mesh, in_specs=(spec,) * 4, out_specs=(spec,) * 4, check_vma=False
    )
```

```python
import functools
import math

import jax
import jax.numpy as jnp
from jax import lax
from jax.experimental import pallas as pl
from jax.experimental.pallas import tpu as pltpu
from jax.sharding import PartitionSpec as P

MESH = pl.DeviceIdType.MESH
HD = 64
HEADS = 15
TOK = 256
HCOL = HEADS * HD
ROWS = 232
PAD = 240
SEGMENT = 5
CHUNK = 80
MASKED = -1e30
BF = jnp.bfloat16
F32 = jnp.float32


def device(zh, x, c, y, zl):
    return (zh * 8 + x * 2 + c, y * 2 + zl)


def kernel(
    q_t, kv, w_in, cot_ref,
    out_o, gq_o, gkv_o, gw_o,
    kv_t, cz, cot_all, w_all, att_all, probs, w_t,
    o_part, o_recv, rx, rz, g_part, g_core, g_recv, a_part, a_recv, gkv_acc,
    wl_s, wl_r, zl_s, zl_r, xa_s, xa_r, yg_s, yg_r, zg_s, zg_r, wc_s, wc_r, xg_s, xg_r,
    yr_s, yr_r, xo_s, xo_r, zo_s, zo_r, gc_s, gc_r, zr_s, zr_r, ar_s, ar_r,
):
    dp = lax.axis_index("dp")
    tensor = lax.axis_index("tensor")
    zh, x, c = dp // 8, (dp // 2) % 4, dp % 2
    y, zl = tensor // 2, tensor % 2
    sign = 1 - 2 * c
    x_p, x_m, x_2 = (x + 4 + sign) % 4, (x + 4 - sign) % 4, (x + 2) % 4
    y_p, y_m, y_2 = (y + 4 + sign) % 4, (y + 4 - sign) % 4, (y + 2) % 4
    z_p, z_m, z_2 = (zh + 4 + sign) % 4, (zh + 4 - sign) % 4, (zh + 2) % 4
    at_x = lambda other: device(zh, other, c, y, zl)
    at_y = lambda other: device(zh, x, c, other, zl)
    at_z = lambda other: device(other, x, c, y, zl)
    sibling = device(zh, x, 1 - c, y, zl)
    partner = device(zh, x, c, y, 1 - zl)

    def send(src, dst, send_sem, recv_sem, to):
        return pltpu.make_async_remote_copy(
            src_ref=src, dst_ref=dst, send_sem=send_sem, recv_sem=recv_sem,
            device_id=to, device_id_type=MESH,
        )

    started = []

    def start(*args):
        copy = send(*args)
        copy.start()
        started.append(copy)
        return copy

    barrier = pltpu.get_barrier_semaphore()
    others = [sibling, partner, at_x(x_p), at_x(x_m), at_x(x_2)]
    others += [at_y(y_p), at_y(y_m), at_z(z_p), at_z(z_m)]
    for other in others:
        pl.semaphore_signal(barrier, inc=1, device_id=other, device_id_type=MESH)
    pl.semaphore_wait(barrier, len(others))

    turned = cot_ref[...].astype(F32)
    zl_copy = []
    for r in range(2):
        for h in range(2):
            first = (2 * h + r) * ROWS
            cz[zl, r, h, pl.ds(PAD - 16, 16)] = jnp.zeros((16, TOK), BF)
            cz[zl, r, h, pl.ds(0, ROWS)] = turned[first : first + ROWS].astype(BF)
        block = cz.at[zl, r]
        zl_copy.append(start(block, block, zl_s.at[r], zl_r.at[r], partner))
    kv_t[...] = jnp.transpose(kv[...])
    w_all[zh, c, pl.ds(PAD - 16, 16)] = jnp.zeros((16, HCOL), BF)
    w_all[zh, c, pl.ds(0, ROWS)] = w_in[...]

    row = lax.broadcasted_iota(jnp.int32, (TOK, TOK), 0)
    col = lax.broadcasted_iota(jnp.int32, (TOK, TOK), 1)
    allowed = row <= col
    scale = 1.0 / math.sqrt(HD)

    def forward_head(h, carry):
        rows = pl.ds(pl.multiple_of(h * HD, HD), HD)
        scores = jnp.dot(kv[:, :HD], q_t[rows, :], preferred_element_type=F32)
        scores = jnp.where(allowed, scores * scale, MASKED)
        lifted = jnp.exp(scores - jnp.max(scores, axis=0, keepdims=True))
        soft = lifted / jnp.sum(lifted, axis=0, keepdims=True)
        probs[h] = soft
        attended = jnp.dot(kv_t[HD:, :], soft.astype(BF), preferred_element_type=F32)
        att_all[x, rows, :] = attended.astype(BF)
        return carry

    def attention_segment(k):
        lax.fori_loop(k * SEGMENT, (k + 1) * SEGMENT, forward_head, 0)

    def a2a_start(r):
        copies = {}
        for d in (2, 1, 3):
            to = (x + d) % 4
            copies[d] = start(
                cz.at[to // 2, r, to % 2], cot_all.at[y, x, r],
                xa_s.at[r, d - 1], xa_r.at[r, d - 1], at_x(to),
            )
        cot_all[y, x, r] = cz[x // 2, r, x % 2]
        return copies

    def y_start(r, d):
        block = cot_all.at[y, (x + 4 - d) % 4, r]
        return (
            start(block, block, yg_s.at[0, r, d], yg_r.at[0, r, d], at_y(y_p)),
            start(block, block, yg_s.at[1, r, d], yg_r.at[1, r, d], at_y(y_m)),
        )

    def y_forward(r, d):
        yg[r, d][0].wait_recv()
        block = cot_all.at[y_m, (x + 4 - d) % 4, r]
        yf.append(start(block, block, yg_s.at[2, r, d], yg_r.at[2, r, d], at_y(y_p)))

    def w_rows(z, i):
        return w_all.at[z, c, pl.ds(i * CHUNK, CHUNK)]

    def w_core(z):
        block = w_all.at[z, c]
        return start(block, block, wc_s.at[z], wc_r.at[z], sibling)

    wg, w_c = [], []

    def w_start():
        for i in range(3):
            block = w_rows(zh, i)
            wg.append((
                start(block, block, zg_s.at[0, i], zg_r.at[0, i], at_z(z_p)),
                start(block, block, zg_s.at[1, i], zg_r.at[1, i], at_z(z_m)),
            ))
        w_c.append(w_core(zh))

    attention_segment(0)
    attention_segment(1)
    yg, yf, xa = {}, [], {}
    zl_copy[0].wait_recv()
    xa[0] = a2a_start(0)
    yg[0, 0] = y_start(0, 0)
    attention_segment(2)
    zl_copy[1].wait_recv()
    xa[1] = a2a_start(1)
    w_start()
    for d in (1, 3, 2):
        xa[0][d].wait_recv()
        yg[0, d] = y_start(0, d)
    yg[1, 0] = y_start(1, 0)
    y_forward(0, 0)
    for d in (1, 3, 2):
        xa[1][d].wait_recv()
        yg[1, d] = y_start(1, d)
        y_forward(0, d)
    att_copies = []
    for k in range(3):
        part = att_all.at[x, pl.ds(k * SEGMENT * HD, SEGMENT * HD)]
        att_copies.append((
            start(part, part, xg_s.at[0, k], xg_r.at[0, k], at_x(x_p)),
            start(part, part, xg_s.at[1, k], xg_r.at[1, k], at_x(x_m)),
        ))
    y_forward(1, 0)
    w_f, forwarded = [], []
    for i, d in enumerate((1, 3, 2)):
        wg[i][0].wait_recv()
        block = w_rows(z_m, i)
        w_f.append(start(block, block, zg_s.at[2, i], zg_r.at[2, i], at_z(z_p)))
        y_forward(1, d)
        att_copies[i][0].wait_recv()
        part = att_all.at[x_m, pl.ds(i * SEGMENT * HD, SEGMENT * HD)]
        forwarded.append(start(part, part, xg_s.at[2, i], xg_r.at[2, i], at_x(x_p)))
    w_c.append(w_core(z_m))
    for i in range(3):
        wg[i][1].wait_recv()
    w_c.append(w_core(z_p))
    for k in range(3):
        att_copies[k][1].wait_recv()
        forwarded[k].wait_recv()

    def out_partial(dest):
        weight = w_all[dest].reshape(2 * PAD, HCOL)

        def one(j, carry):
            value = jnp.dot(weight, att_all[j], preferred_element_type=F32)
            o_part[dest, j] = value.astype(BF).reshape(2, PAD, TOK)
            return carry

        lax.fori_loop(0, 4, one, 0)

    def transpose_weight(k):
        w_t[k] = jnp.transpose(w_all[k].reshape(2 * PAD, HCOL))

    def weight_partial(dest):
        total = jnp.zeros((2 * PAD, HCOL), F32)
        for j in range(4):
            total += lax.dot_general(
                cot_all[dest, j].reshape(2 * PAD, TOK), att_all[j],
                (((1,), (1,)), ((), ())), preferred_element_type=F32,
            )
        g_part[dest] = (total * (1.0 / TOK)).astype(BF).reshape(2, PAD, HCOL)

    gc = []

    def weight_step(k, dest):
        weight_partial(dest)
        gc.append(start(g_part.at[dest, 1 - c], g_core.at[dest], gc_s.at[dest], gc_r.at[dest], sibling))

    def attended_partial(dest):
        total = jnp.zeros((HCOL, TOK), F32)
        for k in range(4):
            total += jnp.dot(w_t[k], cot_all[k, dest].reshape(2 * PAD, TOK), preferred_element_type=F32)
        a_part[dest] = total.astype(BF)

    def add_out(dest, kind, j):
        value = o_part[dest, j].astype(F32) + o_recv[kind, j].astype(F32)
        o_part[dest, j] = value.astype(BF)

    ORDER = (2, 1, 3, 0)

    yr2 = {}

    def y_middle(d):
        yr0[d].wait_recv()
        add_out(y_m, 0, (x + d) % 4)
        yr2[d] = y_copy(2, d)
        yr2[d].start()
        started.append(yr2[d])

    def weight_join(dest, i):
        rows = pl.ds(i * CHUNK, CHUNK)
        value = g_part[dest, c, rows].astype(F32) + g_core[dest, rows].astype(F32)
        return rows, value

    def z_reduce(kind, i, dest, to):
        rows = pl.ds(i * CHUNK, CHUNK)
        return start(
            g_part.at[dest, c, rows], g_recv.at[kind, rows],
            zr_s.at[kind, i], zr_r.at[kind, i], at_z(to),
        )

    def y_copy(kind, d):
        dest, to = ((y_2, y_m), (y_p, y_p), (y_m, y_m))[kind]
        j = (x + d) % 4
        return send(o_part.at[dest, j], o_recv.at[kind, j], yr_s.at[kind, d], yr_r.at[kind, d], at_y(to))

    def out_start(z):
        for kind, dest in ((0, y_2), (1, y_p)):
            @pl.when(z == dest)
            def _():
                for d in ORDER:
                    y_copy(kind, d).start()

    for i, z in enumerate((zh, z_m, z_p)):
        w_c[i].wait_recv()
        out_partial(z)
        transpose_weight(z)
    for pair in yg.values():
        pair[1].wait_recv()
    for copy in yf:
        copy.wait_recv()
    for z in (zh, z_m, z_p):
        out_start(z)
    weight_step(0, z_2)
    last = []
    for i in range(3):
        w_f[i].wait_recv()
        block = w_rows(z_2, i)
        last.append(start(block, block, wl_s.at[i], wl_r.at[i], sibling))
    weight_step(1, z_p)
    zr0 = []
    gc[0].wait_recv()
    for i in range(3):
        rows, value = weight_join(z_2, i)
        g_part[z_2, c, rows] = value.astype(BF)
        zr0.append(z_reduce(0, i, z_2, z_m))
    for copy in last:
        copy.wait_recv()
    out_partial(z_2)
    out_start(z_2)
    yr0 = {d: y_copy(0, d) for d in ORDER}
    yr1 = {d: y_copy(1, d) for d in ORDER}
    started.extend(yr0.values())
    started.extend(yr1.values())
    transpose_weight(z_2)
    attended_partial(x_2)
    ar0 = start(a_part.at[x_2], a_recv.at[0], ar_s.at[0], ar_r.at[0], at_x(x_m))
    y_middle(2)
    weight_step(2, z_m)
    gc[1].wait_recv()
    zr1 = []
    for i in range(3):
        rows, value = weight_join(z_p, i)
        g_part[z_p, c, rows] = value.astype(BF)
        zr1.append(z_reduce(1, i, z_p, z_p))
    y_middle(1)
    attended_partial(x_p)
    ar1 = start(a_part.at[x_p], a_recv.at[1], ar_s.at[1], ar_r.at[1], at_x(x_p))
    y_middle(3)
    attended_partial(x_m)
    ar0.wait_recv()
    a_part[x_m] = (a_part[x_m].astype(F32) + a_recv[0].astype(F32)).astype(BF)
    ar2 = start(a_part.at[x_m], a_recv.at[2], ar_s.at[2], ar_r.at[2], at_x(x_m))
    y_middle(0)
    gc[2].wait_recv()
    zr2 = []
    for i in range(3):
        zr0[i].wait_recv()
        rows, value = weight_join(z_m, i)
        g_part[z_m, c, rows] = (value + g_recv[0, rows].astype(F32)).astype(BF)
        zr2.append(z_reduce(2, i, z_m, z_m))
    weight_step(3, zh)
    attended_partial(x)

    def out_final(j):
        value = o_part[y, j].astype(F32) + o_recv[1, j].astype(F32) + o_recv[2, j].astype(F32)
        return value.astype(BF)

    xo = []

    def out_send(d):
        to = (x + d) % 4
        yr1[d].wait_recv()
        yr2[d].wait_recv()
        o_part[y, to] = out_final(to)
        xo.append(start(o_part.at[y, to], rx.at[x], xo_s.at[d - 1], xo_r.at[d - 1], at_x(to)))

    gkv_acc[...] = jnp.zeros_like(gkv_acc)

    def backward_head(h, carry):
        rows = pl.ds(pl.multiple_of(h * HD, HD), HD)
        grad = a_part[x, rows, :]
        soft = probs[h]
        grad_p = jnp.dot(kv[:, HD:], grad, preferred_element_type=F32)
        dot = jnp.sum(soft * grad_p, axis=0, keepdims=True)
        grad_s = (soft * (grad_p - dot) * scale).astype(BF)
        gq_o[rows, :] = jnp.dot(kv_t[:HD, :], grad_s, preferred_element_type=F32).astype(BF)
        last = (((1,), (1,)), ((), ()))
        gkv_acc[:HD, :] += lax.dot_general(q_t[rows, :], grad_s, last, preferred_element_type=F32)
        gkv_acc[HD:, :] += lax.dot_general(grad, soft.astype(BF), last, preferred_element_type=F32)
        return carry

    def backward(first, past):
        lax.fori_loop(first, past, backward_head, 0)

    out_send(2)
    ar1.wait_recv()
    ar2.wait_recv()
    a_part[x] = (
        a_part[x].astype(F32) + a_recv[1].astype(F32) + a_recv[2].astype(F32)
    ).astype(BF)
    backward(0, 4)
    out_send(1)
    out_send(3)
    backward(4, 8)
    yr1[0].wait_recv()
    yr2[0].wait_recv()
    rx[x] = out_final(x)

    def zo_send(src):
        h = src % 2
        copy = send(rx.at[src], rz.at[h], zo_s.at[h], zo_r.at[h], partner)

        @pl.when(src // 2 != zl)
        def _():
            copy.start()

    zo_send(x)
    for copy, d in zip(xo, (2, 1, 3)):
        copy.wait_recv()
        zo_send((x + 4 - d) % 4)
    backward(8, HEADS)
    gkv_o[...] = jnp.transpose(gkv_acc[...]).astype(BF)
    gc[3].wait_recv()
    for i in range(3):
        zr1[i].wait_recv()
        zr2[i].wait_recv()
        rows, value = weight_join(zh, i)
        value += g_recv[1, rows].astype(F32) + g_recv[2, rows].astype(F32)
        if i < 2:
            gw_o[rows] = value.astype(BF)
        else:
            gw_o[pl.ds(2 * CHUNK, ROWS - 2 * CHUNK)] = value[: ROWS - 2 * CHUNK].astype(BF)

    for h in range(2):
        copy = send(rx.at[2 * (1 - zl) + h], rz.at[h], zo_s.at[h], zo_r.at[h], partner)
        copy.wait_recv()
        copy.wait_send()
    value = [
        (rx[2 * zl + q // 2, q % 2].astype(F32) + rz[q // 2, q % 2].astype(F32))[:ROWS]
        for q in range(4)
    ]
    out_o[...] = jnp.concatenate(value, axis=0).astype(BF)
    for copy in started:
        copy.wait_send()


def body(queries, keys_values, out_weight, cotangent):
    vmem = pl.BlockSpec(memory_space=pltpu.VMEM)
    dma = lambda *shape: pltpu.SemaphoreType.DMA(shape)
    scratch = [
        pltpu.VMEM((2 * HD, TOK), BF),
        pltpu.VMEM((2, 2, 2, PAD, TOK), BF),
        pltpu.VMEM((4, 4, 2, PAD, TOK), BF),
        pltpu.VMEM((4, 2, PAD, HCOL), BF),
        pltpu.VMEM((4, HCOL, TOK), BF),
        pltpu.VMEM((HEADS, TOK, TOK), F32),
        pltpu.VMEM((4, HCOL, 2 * PAD), BF),
        pltpu.VMEM((4, 4, 2, PAD, TOK), BF),
        pltpu.VMEM((3, 4, 2, PAD, TOK), BF),
        pltpu.VMEM((4, 2, PAD, TOK), BF),
        pltpu.VMEM((2, 2, PAD, TOK), BF),
        pltpu.VMEM((4, 2, PAD, HCOL), BF),
        pltpu.VMEM((4, PAD, HCOL), BF),
        pltpu.VMEM((3, PAD, HCOL), BF),
        pltpu.VMEM((4, HCOL, TOK), BF),
        pltpu.VMEM((3, HCOL, TOK), BF),
        pltpu.VMEM((2 * HD, TOK), F32),
        dma(3), dma(3), dma(2), dma(2), dma(2, 3), dma(2, 3), dma(3, 2, 4), dma(3, 2, 4), dma(3, 3), dma(3, 3), dma(4), dma(4),
        dma(3, 3), dma(3, 3), dma(3, 4), dma(3, 4), dma(3), dma(3), dma(2), dma(2),
        dma(4), dma(4), dma(3, 3), dma(3, 3), dma(3), dma(3),
    ]
    out, gq, gkv, gw = pl.pallas_call(
        kernel,
        out_shape=(
            jax.ShapeDtypeStruct((4 * ROWS, TOK), BF),
            jax.ShapeDtypeStruct((HCOL, TOK), BF),
            jax.ShapeDtypeStruct((TOK, 2 * HD), BF),
            jax.ShapeDtypeStruct((ROWS, HCOL), BF),
        ),
        in_specs=[vmem] * 4,
        out_specs=(vmem,) * 4,
        scratch_shapes=scratch,
        compiler_params=pltpu.CompilerParams(
            collective_id=0, has_side_effects=True, vmem_limit_bytes=60 * 2**20
        ),
        cost_estimate=pl.CostEstimate(flops=12 * 10**9, bytes_accessed=5 * 10**6, transcendentals=10**6),
    )(queries.T, keys_values, out_weight, cotangent.T)
    return out.T, gq.T, gkv, gw


def solution(mesh):
    spec = P("dp", "tensor")
    return jax.shard_map(
        body, mesh=mesh, in_specs=(spec,) * 4, out_specs=(spec,) * 4, check_vma=False
    )
```

```python
import functools
import math

import jax
import jax.numpy as jnp
from jax import lax
from jax.experimental import pallas as pl
from jax.experimental.pallas import tpu as pltpu
from jax.sharding import PartitionSpec as P

MESH = pl.DeviceIdType.MESH
HD = 64
HEADS = 15
TOK = 256
HCOL = HEADS * HD
ROWS = 232
PAD = 240
SEGMENT = 5
CHUNK = 80
MASKED = -1e30
BF = jnp.bfloat16
F32 = jnp.float32


def device(zh, x, c, y, zl):
    return (zh * 8 + x * 2 + c, y * 2 + zl)


def kernel(
    q_t, kv, w_in, cot_ref,
    out_o, gq_o, gkv_o, gw_o,
    kv_t, cz, cot_all, w_all, att_all, probs, w_t,
    o_part, o_recv, rx, rz, g_part, g_core, g_recv, a_part, a_recv, gkv_acc,
    wl_s, wl_r, zl_s, zl_r, xa_s, xa_r, yg_s, yg_r, zg_s, zg_r, wc_s, wc_r, xg_s, xg_r,
    yr_s, yr_r, xo_s, xo_r, zo_s, zo_r, gc_s, gc_r, zr_s, zr_r, ar_s, ar_r,
):
    dp = lax.axis_index("dp")
    tensor = lax.axis_index("tensor")
    zh, x, c = dp // 8, (dp // 2) % 4, dp % 2
    y, zl = tensor // 2, tensor % 2
    sign = 1 - 2 * c
    x_p, x_m, x_2 = (x + 4 + sign) % 4, (x + 4 - sign) % 4, (x + 2) % 4
    y_p, y_m, y_2 = (y + 4 + sign) % 4, (y + 4 - sign) % 4, (y + 2) % 4
    z_p, z_m, z_2 = (zh + 4 + sign) % 4, (zh + 4 - sign) % 4, (zh + 2) % 4
    at_x = lambda other: device(zh, other, c, y, zl)
    at_y = lambda other: device(zh, x, c, other, zl)
    at_z = lambda other: device(other, x, c, y, zl)
    sibling = device(zh, x, 1 - c, y, zl)
    partner = device(zh, x, c, y, 1 - zl)

    def send(src, dst, send_sem, recv_sem, to):
        return pltpu.make_async_remote_copy(
            src_ref=src, dst_ref=dst, send_sem=send_sem, recv_sem=recv_sem,
            device_id=to, device_id_type=MESH,
        )

    started = []

    def start(*args):
        copy = send(*args)
        copy.start()
        started.append(copy)
        return copy

    barrier = pltpu.get_barrier_semaphore()
    others = [sibling, partner, at_x(x_p), at_x(x_m), at_x(x_2)]
    others += [at_y(y_p), at_y(y_m), at_z(z_p), at_z(z_m)]
    for other in others:
        pl.semaphore_signal(barrier, inc=1, device_id=other, device_id_type=MESH)
    pl.semaphore_wait(barrier, len(others))

    turned = cot_ref[...].astype(F32)
    zl_copy = []
    for r in range(2):
        for h in range(2):
            first = (2 * h + r) * ROWS
            cz[zl, r, h, pl.ds(PAD - 16, 16)] = jnp.zeros((16, TOK), BF)
            cz[zl, r, h, pl.ds(0, ROWS)] = turned[first : first + ROWS].astype(BF)
        block = cz.at[zl, r]
        zl_copy.append(start(block, block, zl_s.at[r], zl_r.at[r], partner))
    kv_t[...] = jnp.transpose(kv[...])
    w_all[zh, c, pl.ds(PAD - 16, 16)] = jnp.zeros((16, HCOL), BF)
    w_all[zh, c, pl.ds(0, ROWS)] = w_in[...]

    row = lax.broadcasted_iota(jnp.int32, (TOK, TOK), 0)
    col = lax.broadcasted_iota(jnp.int32, (TOK, TOK), 1)
    allowed = row <= col
    scale = 1.0 / math.sqrt(HD)

    def forward_head(h, carry):
        rows = pl.ds(pl.multiple_of(h * HD, HD), HD)
        scores = jnp.dot(kv[:, :HD], q_t[rows, :], preferred_element_type=F32)
        scores = jnp.where(allowed, scores * scale, MASKED)
        lifted = jnp.exp(scores - jnp.max(scores, axis=0, keepdims=True))
        soft = lifted / jnp.sum(lifted, axis=0, keepdims=True)
        probs[h] = soft
        attended = jnp.dot(kv_t[HD:, :], soft.astype(BF), preferred_element_type=F32)
        att_all[x, rows, :] = attended.astype(BF)
        return carry

    def attention_segment(k):
        lax.fori_loop(k * SEGMENT, (k + 1) * SEGMENT, forward_head, 0)

    def a2a_start(r):
        copies = {}
        for d in (2, 1, 3):
            to = (x + d) % 4
            copies[d] = start(
                cz.at[to // 2, r, to % 2], cot_all.at[y, x, r],
                xa_s.at[r, d - 1], xa_r.at[r, d - 1], at_x(to),
            )
        cot_all[y, x, r] = cz[x // 2, r, x % 2]
        return copies

    def y_start(r, d):
        block = cot_all.at[y, (x + 4 - d) % 4, r]
        return (
            start(block, block, yg_s.at[0, r, d], yg_r.at[0, r, d], at_y(y_p)),
            start(block, block, yg_s.at[1, r, d], yg_r.at[1, r, d], at_y(y_m)),
        )

    def y_forward(r, d):
        yg[r, d][0].wait_recv()
        block = cot_all.at[y_m, (x + 4 - d) % 4, r]
        yf.append(start(block, block, yg_s.at[2, r, d], yg_r.at[2, r, d], at_y(y_p)))

    def w_rows(z, i):
        return w_all.at[z, c, pl.ds(i * CHUNK, CHUNK)]

    def w_core(z):
        block = w_all.at[z, c]
        return start(block, block, wc_s.at[z], wc_r.at[z], sibling)

    wg, w_c = [], []

    def w_start():
        for i in range(3):
            block = w_rows(zh, i)
            wg.append((
                start(block, block, zg_s.at[0, i], zg_r.at[0, i], at_z(z_p)),
                start(block, block, zg_s.at[1, i], zg_r.at[1, i], at_z(z_m)),
            ))
        w_c.append(w_core(zh))

    att_copies = []

    def att_start():
        for k in range(3):
            part = att_all.at[x, pl.ds(k * SEGMENT * HD, SEGMENT * HD)]
            att_copies.append((
                start(part, part, xg_s.at[0, k], xg_r.at[0, k], at_x(x_p)),
                start(part, part, xg_s.at[1, k], xg_r.at[1, k], at_x(x_m)),
            ))

    attention_segment(0)
    attention_segment(1)
    yg, yf, xa = {}, [], {}
    zl_copy[0].wait_recv()
    xa[0] = a2a_start(0)
    yg[0, 0] = y_start(0, 0)
    attention_segment(2)
    zl_copy[1].wait_recv()
    xa[1] = a2a_start(1)
    w_start()
    att_start()
    for d in (1, 3, 2):
        xa[0][d].wait_recv()
        yg[0, d] = y_start(0, d)
    yg[1, 0] = y_start(1, 0)
    y_forward(0, 0)
    for d in (1, 3, 2):
        xa[1][d].wait_recv()
        yg[1, d] = y_start(1, d)
        y_forward(0, d)
    y_forward(1, 0)
    w_f, forwarded = [], []

    def w_forward(i):
        wg[i][0].wait_recv()
        block = w_rows(z_m, i)
        w_f.append(start(block, block, zg_s.at[2, i], zg_r.at[2, i], at_z(z_p)))

    def att_forward(i):
        att_copies[i][0].wait_recv()
        part = att_all.at[x_m, pl.ds(i * SEGMENT * HD, SEGMENT * HD)]
        forwarded.append(start(part, part, xg_s.at[2, i], xg_r.at[2, i], at_x(x_p)))

    att_forward(0)
    w_forward(0)
    att_forward(1)
    y_forward(1, 1)
    att_forward(2)
    w_forward(1)
    y_forward(1, 3)
    w_forward(2)
    y_forward(1, 2)
    w_c.append(w_core(z_m))
    for k in range(3):
        att_copies[k][1].wait_recv()
        forwarded[k].wait_recv()

    def out_partial(dest):
        weight = w_all[dest].reshape(2 * PAD, HCOL)

        def one(j, carry):
            value = jnp.dot(weight, att_all[j], preferred_element_type=F32)
            o_part[dest, j] = value.astype(BF).reshape(2, PAD, TOK)
            return carry

        lax.fori_loop(0, 4, one, 0)

    def transpose_weight(k):
        w_t[k] = jnp.transpose(w_all[k].reshape(2 * PAD, HCOL))

    def weight_partial(dest):
        total = jnp.zeros((2 * PAD, HCOL), F32)
        for j in range(4):
            total += lax.dot_general(
                cot_all[dest, j].reshape(2 * PAD, TOK), att_all[j],
                (((1,), (1,)), ((), ())), preferred_element_type=F32,
            )
        g_part[dest] = (total * (1.0 / TOK)).astype(BF).reshape(2, PAD, HCOL)

    gc = []

    def weight_step(k, dest):
        weight_partial(dest)
        gc.append(start(g_part.at[dest, 1 - c], g_core.at[dest], gc_s.at[dest], gc_r.at[dest], sibling))

    def attended_partial(dest):
        total = jnp.zeros((HCOL, TOK), F32)
        for k in range(4):
            total += jnp.dot(w_t[k], cot_all[k, dest].reshape(2 * PAD, TOK), preferred_element_type=F32)
        a_part[dest] = total.astype(BF)

    def add_out(dest, kind, j):
        value = o_part[dest, j].astype(F32) + o_recv[kind, j].astype(F32)
        o_part[dest, j] = value.astype(BF)

    ORDER = (2, 1, 3, 0)

    yr2 = {}

    def y_middle(d):
        yr0[d].wait_recv()
        add_out(y_m, 0, (x + d) % 4)
        yr2[d] = y_copy(2, d)
        yr2[d].start()
        started.append(yr2[d])

    def weight_join(dest, i):
        rows = pl.ds(i * CHUNK, CHUNK)
        value = g_part[dest, c, rows].astype(F32) + g_core[dest, rows].astype(F32)
        return rows, value

    def z_reduce(kind, i, dest, to):
        rows = pl.ds(i * CHUNK, CHUNK)
        return start(
            g_part.at[dest, c, rows], g_recv.at[kind, rows],
            zr_s.at[kind, i], zr_r.at[kind, i], at_z(to),
        )

    def y_copy(kind, d):
        dest, to = ((y_2, y_m), (y_p, y_p), (y_m, y_m))[kind]
        j = (x + d) % 4
        return send(o_part.at[dest, j], o_recv.at[kind, j], yr_s.at[kind, d], yr_r.at[kind, d], at_y(to))

    def out_start(z):
        for kind, dest in ((0, y_2), (1, y_p)):
            @pl.when(z == dest)
            def _():
                for d in ORDER:
                    y_copy(kind, d).start()

    for i, z in enumerate((zh, z_m, z_p)):
        if i == 1:
            for k in range(3):
                wg[k][1].wait_recv()
            w_c.append(w_core(z_p))
        w_c[i].wait_recv()
        out_partial(z)
        out_start(z)
        transpose_weight(z)
    for pair in yg.values():
        pair[1].wait_recv()
    for copy in yf:
        copy.wait_recv()
    weight_step(0, z_2)
    last = []
    for i in range(3):
        w_f[i].wait_recv()
        block = w_rows(z_2, i)
        last.append(start(block, block, wl_s.at[i], wl_r.at[i], sibling))
    weight_step(1, z_p)
    zr0 = []
    gc[0].wait_recv()
    for i in range(3):
        rows, value = weight_join(z_2, i)
        g_part[z_2, c, rows] = value.astype(BF)
        zr0.append(z_reduce(0, i, z_2, z_m))
    for copy in last:
        copy.wait_recv()
    out_partial(z_2)
    out_start(z_2)
    yr0 = {d: y_copy(0, d) for d in ORDER}
    yr1 = {d: y_copy(1, d) for d in ORDER}
    started.extend(yr0.values())
    started.extend(yr1.values())
    transpose_weight(z_2)
    attended_partial(x_2)
    ar0 = start(a_part.at[x_2], a_recv.at[0], ar_s.at[0], ar_r.at[0], at_x(x_m))
    y_middle(2)
    weight_step(2, z_m)
    gc[1].wait_recv()
    zr1 = []
    for i in range(3):
        rows, value = weight_join(z_p, i)
        g_part[z_p, c, rows] = value.astype(BF)
        zr1.append(z_reduce(1, i, z_p, z_p))
    y_middle(1)
    attended_partial(x_p)
    ar1 = start(a_part.at[x_p], a_recv.at[1], ar_s.at[1], ar_r.at[1], at_x(x_p))
    y_middle(3)
    attended_partial(x_m)
    ar0.wait_recv()
    a_part[x_m] = (a_part[x_m].astype(F32) + a_recv[0].astype(F32)).astype(BF)
    ar2 = start(a_part.at[x_m], a_recv.at[2], ar_s.at[2], ar_r.at[2], at_x(x_m))
    y_middle(0)
    gc[2].wait_recv()
    zr2 = []
    for i in range(3):
        zr0[i].wait_recv()
        rows, value = weight_join(z_m, i)
        g_part[z_m, c, rows] = (value + g_recv[0, rows].astype(F32)).astype(BF)
        zr2.append(z_reduce(2, i, z_m, z_m))
    weight_step(3, zh)
    attended_partial(x)

    def out_final(j):
        value = o_part[y, j].astype(F32) + o_recv[1, j].astype(F32) + o_recv[2, j].astype(F32)
        return value.astype(BF)

    xo = []

    def out_send(d):
        to = (x + d) % 4
        yr1[d].wait_recv()
        yr2[d].wait_recv()
        o_part[y, to] = out_final(to)
        xo.append(start(o_part.at[y, to], rx.at[x], xo_s.at[d - 1], xo_r.at[d - 1], at_x(to)))

    gkv_acc[...] = jnp.zeros_like(gkv_acc)

    def backward_head(h, carry):
        rows = pl.ds(pl.multiple_of(h * HD, HD), HD)
        grad = a_part[x, rows, :]
        soft = probs[h]
        grad_p = jnp.dot(kv[:, HD:], grad, preferred_element_type=F32)
        dot = jnp.sum(soft * grad_p, axis=0, keepdims=True)
        grad_s = (soft * (grad_p - dot) * scale).astype(BF)
        gq_o[rows, :] = jnp.dot(kv_t[:HD, :], grad_s, preferred_element_type=F32).astype(BF)
        last = (((1,), (1,)), ((), ()))
        gkv_acc[:HD, :] += lax.dot_general(q_t[rows, :], grad_s, last, preferred_element_type=F32)
        gkv_acc[HD:, :] += lax.dot_general(grad, soft.astype(BF), last, preferred_element_type=F32)
        return carry

    def backward(first, past):
        lax.fori_loop(first, past, backward_head, 0)

    out_send(2)
    ar1.wait_recv()
    ar2.wait_recv()
    a_part[x] = (
        a_part[x].astype(F32) + a_recv[1].astype(F32) + a_recv[2].astype(F32)
    ).astype(BF)
    backward(0, 4)
    out_send(1)
    out_send(3)
    backward(4, 8)
    yr1[0].wait_recv()
    yr2[0].wait_recv()
    rx[x] = out_final(x)

    def zo_send(src):
        h = src % 2
        copy = send(rx.at[src], rz.at[h], zo_s.at[h], zo_r.at[h], partner)

        @pl.when(src // 2 != zl)
        def _():
            copy.start()

    zo_send(x)
    for copy, d in zip(xo, (2, 1, 3)):
        copy.wait_recv()
        zo_send((x + 4 - d) % 4)
    backward(8, HEADS)
    gkv_o[...] = jnp.transpose(gkv_acc[...]).astype(BF)
    gc[3].wait_recv()
    for i in range(3):
        zr1[i].wait_recv()
        zr2[i].wait_recv()
        rows, value = weight_join(zh, i)
        value += g_recv[1, rows].astype(F32) + g_recv[2, rows].astype(F32)
        if i < 2:
            gw_o[rows] = value.astype(BF)
        else:
            gw_o[pl.ds(2 * CHUNK, ROWS - 2 * CHUNK)] = value[: ROWS - 2 * CHUNK].astype(BF)

    for h in range(2):
        copy = send(rx.at[2 * (1 - zl) + h], rz.at[h], zo_s.at[h], zo_r.at[h], partner)
        copy.wait_recv()
        copy.wait_send()
    value = [
        (rx[2 * zl + q // 2, q % 2].astype(F32) + rz[q // 2, q % 2].astype(F32))[:ROWS]
        for q in range(4)
    ]
    out_o[...] = jnp.concatenate(value, axis=0).astype(BF)
    for copy in started:
        copy.wait_send()


def body(queries, keys_values, out_weight, cotangent):
    vmem = pl.BlockSpec(memory_space=pltpu.VMEM)
    dma = lambda *shape: pltpu.SemaphoreType.DMA(shape)
    scratch = [
        pltpu.VMEM((2 * HD, TOK), BF),
        pltpu.VMEM((2, 2, 2, PAD, TOK), BF),
        pltpu.VMEM((4, 4, 2, PAD, TOK), BF),
        pltpu.VMEM((4, 2, PAD, HCOL), BF),
        pltpu.VMEM((4, HCOL, TOK), BF),
        pltpu.VMEM((HEADS, TOK, TOK), F32),
        pltpu.VMEM((4, HCOL, 2 * PAD), BF),
        pltpu.VMEM((4, 4, 2, PAD, TOK), BF),
        pltpu.VMEM((3, 4, 2, PAD, TOK), BF),
        pltpu.VMEM((4, 2, PAD, TOK), BF),
        pltpu.VMEM((2, 2, PAD, TOK), BF),
        pltpu.VMEM((4, 2, PAD, HCOL), BF),
        pltpu.VMEM((4, PAD, HCOL), BF),
        pltpu.VMEM((3, PAD, HCOL), BF),
        pltpu.VMEM((4, HCOL, TOK), BF),
        pltpu.VMEM((3, HCOL, TOK), BF),
        pltpu.VMEM((2 * HD, TOK), F32),
        dma(3), dma(3), dma(2), dma(2), dma(2, 3), dma(2, 3), dma(3, 2, 4), dma(3, 2, 4), dma(3, 3), dma(3, 3), dma(4), dma(4),
        dma(3, 3), dma(3, 3), dma(3, 4), dma(3, 4), dma(3), dma(3), dma(2), dma(2),
        dma(4), dma(4), dma(3, 3), dma(3, 3), dma(3), dma(3),
    ]
    out, gq, gkv, gw = pl.pallas_call(
        kernel,
        out_shape=(
            jax.ShapeDtypeStruct((4 * ROWS, TOK), BF),
            jax.ShapeDtypeStruct((HCOL, TOK), BF),
            jax.ShapeDtypeStruct((TOK, 2 * HD), BF),
            jax.ShapeDtypeStruct((ROWS, HCOL), BF),
        ),
        in_specs=[vmem] * 4,
        out_specs=(vmem,) * 4,
        scratch_shapes=scratch,
        compiler_params=pltpu.CompilerParams(
            collective_id=0, has_side_effects=True, vmem_limit_bytes=60 * 2**20
        ),
        cost_estimate=pl.CostEstimate(flops=12 * 10**9, bytes_accessed=5 * 10**6, transcendentals=10**6),
    )(queries.T, keys_values, out_weight, cotangent.T)
    return out.T, gq.T, gkv, gw


def solution(mesh):
    spec = P("dp", "tensor")
    return jax.shard_map(
        body, mesh=mesh, in_specs=(spec,) * 4, out_specs=(spec,) * 4, check_vma=False
    )
```

```python
import functools
import math

import jax
import jax.numpy as jnp
from jax import lax
from jax.experimental import pallas as pl
from jax.experimental.pallas import tpu as pltpu
from jax.sharding import PartitionSpec as P

MESH = pl.DeviceIdType.MESH
HD = 64
HEADS = 15
TOK = 256
HCOL = HEADS * HD
ROWS = 232
PAD = 240
SEGMENT = 5
CHUNK = 80
MASKED = -1e30
BF = jnp.bfloat16
F32 = jnp.float32


def device(zh, x, c, y, zl):
    return (zh * 8 + x * 2 + c, y * 2 + zl)


def kernel(
    q_t, kv, w_in, cot_ref,
    out_o, gq_o, gkv_o, gw_o,
    kv_t, cz, cot_all, w_all, att_all, probs, w_t,
    o_part, o_recv, rx, rz, g_part, g_core, g_recv, a_part, a_recv, gkv_acc,
    wl_s, wl_r, zl_s, zl_r, xa_s, xa_r, yg_s, yg_r, zg_s, zg_r, wc_s, wc_r, xg_s, xg_r,
    yr_s, yr_r, xo_s, xo_r, zo_s, zo_r, gc_s, gc_r, zr_s, zr_r, ar_s, ar_r,
):
    dp = lax.axis_index("dp")
    tensor = lax.axis_index("tensor")
    zh, x, c = dp // 8, (dp // 2) % 4, dp % 2
    y, zl = tensor // 2, tensor % 2
    sign = 1 - 2 * c
    x_p, x_m, x_2 = (x + 4 + sign) % 4, (x + 4 - sign) % 4, (x + 2) % 4
    y_p, y_m, y_2 = (y + 4 + sign) % 4, (y + 4 - sign) % 4, (y + 2) % 4
    z_p, z_m, z_2 = (zh + 4 + sign) % 4, (zh + 4 - sign) % 4, (zh + 2) % 4
    at_x = lambda other: device(zh, other, c, y, zl)
    at_y = lambda other: device(zh, x, c, other, zl)
    at_z = lambda other: device(other, x, c, y, zl)
    sibling = device(zh, x, 1 - c, y, zl)
    partner = device(zh, x, c, y, 1 - zl)

    def send(src, dst, send_sem, recv_sem, to):
        return pltpu.make_async_remote_copy(
            src_ref=src, dst_ref=dst, send_sem=send_sem, recv_sem=recv_sem,
            device_id=to, device_id_type=MESH,
        )

    started = []

    def start(*args):
        copy = send(*args)
        copy.start()
        started.append(copy)
        return copy

    barrier = pltpu.get_barrier_semaphore()
    others = [sibling, partner, at_x(x_p), at_x(x_m), at_x(x_2)]
    others += [at_y(y_p), at_y(y_m), at_z(z_p), at_z(z_m)]
    for other in others:
        pl.semaphore_signal(barrier, inc=1, device_id=other, device_id_type=MESH)
    pl.semaphore_wait(barrier, len(others))

    turned = cot_ref[...].astype(F32)
    zl_copy = []
    for r in range(2):
        for h in range(2):
            first = (2 * h + r) * ROWS
            cz[zl, r, h, pl.ds(PAD - 16, 16)] = jnp.zeros((16, TOK), BF)
            cz[zl, r, h, pl.ds(0, ROWS)] = turned[first : first + ROWS].astype(BF)
        block = cz.at[zl, r]
        zl_copy.append(start(block, block, zl_s.at[r], zl_r.at[r], partner))
    kv_t[...] = jnp.transpose(kv[...])
    w_all[zh, c, pl.ds(PAD - 16, 16)] = jnp.zeros((16, HCOL), BF)
    w_all[zh, c, pl.ds(0, ROWS)] = w_in[...]

    row = lax.broadcasted_iota(jnp.int32, (TOK, TOK), 0)
    col = lax.broadcasted_iota(jnp.int32, (TOK, TOK), 1)
    allowed = row <= col
    scale = 1.0 / math.sqrt(HD)

    def forward_head(h, carry):
        rows = pl.ds(pl.multiple_of(h * HD, HD), HD)
        scores = jnp.dot(kv[:, :HD], q_t[rows, :], preferred_element_type=F32)
        scores = jnp.where(allowed, scores * scale, MASKED)
        lifted = jnp.exp(scores - jnp.max(scores, axis=0, keepdims=True))
        soft = lifted / jnp.sum(lifted, axis=0, keepdims=True)
        probs[h] = soft
        attended = jnp.dot(kv_t[HD:, :], soft.astype(BF), preferred_element_type=F32)
        att_all[x, rows, :] = attended.astype(BF)
        return carry

    def attention_segment(k):
        lax.fori_loop(k * SEGMENT, (k + 1) * SEGMENT, forward_head, 0)

    def a2a_start(r):
        copies = {}
        for d in (2, 1, 3):
            to = (x + d) % 4
            copies[d] = start(
                cz.at[to // 2, r, to % 2], cot_all.at[y, x, r],
                xa_s.at[r, d - 1], xa_r.at[r, d - 1], at_x(to),
            )
        cot_all[y, x, r] = cz[x // 2, r, x % 2]
        return copies

    def y_start(r, d):
        block = cot_all.at[y, (x + 4 - d) % 4, r]
        return (
            start(block, block, yg_s.at[0, r, d], yg_r.at[0, r, d], at_y(y_p)),
            start(block, block, yg_s.at[1, r, d], yg_r.at[1, r, d], at_y(y_m)),
        )

    def y_forward(r, d):
        yg[r, d][0].wait_recv()
        block = cot_all.at[y_m, (x + 4 - d) % 4, r]
        yf.append(start(block, block, yg_s.at[2, r, d], yg_r.at[2, r, d], at_y(y_p)))

    def w_rows(z, i):
        return w_all.at[z, c, pl.ds(i * CHUNK, CHUNK)]

    def w_core(z):
        block = w_all.at[z, c]
        return start(block, block, wc_s.at[z], wc_r.at[z], sibling)

    wg, w_c = [], []

    def w_start():
        for i in range(3):
            block = w_rows(zh, i)
            wg.append((
                start(block, block, zg_s.at[0, i], zg_r.at[0, i], at_z(z_p)),
                start(block, block, zg_s.at[1, i], zg_r.at[1, i], at_z(z_m)),
            ))
        w_c.append(w_core(zh))

    att_copies = []

    def att_start():
        for k in range(3):
            part = att_all.at[x, pl.ds(k * SEGMENT * HD, SEGMENT * HD)]
            att_copies.append((
                start(part, part, xg_s.at[0, k], xg_r.at[0, k], at_x(x_p)),
                start(part, part, xg_s.at[1, k], xg_r.at[1, k], at_x(x_m)),
            ))

    attention_segment(0)
    attention_segment(1)
    yg, yf, xa = {}, [], {}
    zl_copy[0].wait_recv()
    xa[0] = a2a_start(0)
    yg[0, 0] = y_start(0, 0)
    attention_segment(2)
    zl_copy[1].wait_recv()
    xa[1] = a2a_start(1)
    w_start()
    att_start()
    for d in (1, 3, 2):
        xa[0][d].wait_recv()
        yg[0, d] = y_start(0, d)
    yg[1, 0] = y_start(1, 0)
    y_forward(0, 0)
    for d in (1, 3, 2):
        xa[1][d].wait_recv()
        yg[1, d] = y_start(1, d)
        y_forward(0, d)
    y_forward(1, 0)
    w_f, forwarded = [], []

    def w_forward(i):
        wg[i][0].wait_recv()
        block = w_rows(z_m, i)
        w_f.append(start(block, block, zg_s.at[2, i], zg_r.at[2, i], at_z(z_p)))

    def att_forward(i):
        att_copies[i][0].wait_recv()
        part = att_all.at[x_m, pl.ds(i * SEGMENT * HD, SEGMENT * HD)]
        forwarded.append(start(part, part, xg_s.at[2, i], xg_r.at[2, i], at_x(x_p)))

    att_forward(0)
    w_forward(0)
    att_forward(1)
    y_forward(1, 1)
    att_forward(2)
    w_forward(1)
    y_forward(1, 3)
    w_forward(2)
    y_forward(1, 2)
    w_c.append(w_core(z_m))
    for k in range(3):
        att_copies[k][1].wait_recv()
        forwarded[k].wait_recv()

    def out_partial(dest):
        weight = w_all[dest].reshape(2 * PAD, HCOL)

        def one(j, carry):
            value = jnp.dot(weight, att_all[j], preferred_element_type=F32)
            o_part[dest, j] = value.astype(BF).reshape(2, PAD, TOK)
            return carry

        lax.fori_loop(0, 4, one, 0)

    def transpose_weight(k):
        w_t[k] = jnp.transpose(w_all[k].reshape(2 * PAD, HCOL))

    def weight_partial(dest):
        total = jnp.zeros((2 * PAD, HCOL), F32)
        for j in range(4):
            total += lax.dot_general(
                cot_all[dest, j].reshape(2 * PAD, TOK), att_all[j],
                (((1,), (1,)), ((), ())), preferred_element_type=F32,
            )
        g_part[dest] = (total * (1.0 / TOK)).astype(BF).reshape(2, PAD, HCOL)

    gc = []

    def weight_step(k, dest):
        weight_partial(dest)
        gc.append(start(g_part.at[dest, 1 - c], g_core.at[dest], gc_s.at[dest], gc_r.at[dest], sibling))

    def attended_partial(dest):
        total = jnp.zeros((HCOL, TOK), F32)
        for k in range(4):
            total += jnp.dot(w_t[k], cot_all[k, dest].reshape(2 * PAD, TOK), preferred_element_type=F32)
        a_part[dest] = total.astype(BF)

    def add_out(dest, kind, j):
        value = o_part[dest, j].astype(F32) + o_recv[kind, j].astype(F32)
        o_part[dest, j] = value.astype(BF)

    ORDER = (2, 1, 3, 0)

    yr2 = {}

    def y_middle(d):
        yr0[d].wait_recv()
        add_out(y_m, 0, (x + d) % 4)
        yr2[d] = y_copy(2, d)
        yr2[d].start()
        started.append(yr2[d])

    def weight_join(dest, i):
        rows = pl.ds(i * CHUNK, CHUNK)
        value = g_part[dest, c, rows].astype(F32) + g_core[dest, rows].astype(F32)
        return rows, value

    def z_reduce(kind, i, dest, to):
        rows = pl.ds(i * CHUNK, CHUNK)
        return start(
            g_part.at[dest, c, rows], g_recv.at[kind, rows],
            zr_s.at[kind, i], zr_r.at[kind, i], at_z(to),
        )

    def y_copy(kind, d):
        dest, to = ((y_2, y_m), (y_p, y_p), (y_m, y_m))[kind]
        j = (x + d) % 4
        return send(o_part.at[dest, j], o_recv.at[kind, j], yr_s.at[kind, d], yr_r.at[kind, d], at_y(to))

    def out_start(z):
        for kind, dest in ((0, y_2), (1, y_p)):
            @pl.when(z == dest)
            def _():
                for d in ORDER:
                    y_copy(kind, d).start()

    for i, z in enumerate((zh, z_m, z_p)):
        if i == 1:
            for k in range(3):
                wg[k][1].wait_recv()
            w_c.append(w_core(z_p))
        w_c[i].wait_recv()
        out_partial(z)
        out_start(z)
    for z in (zh, z_m, z_p):
        transpose_weight(z)
    for pair in yg.values():
        pair[1].wait_recv()
    for copy in yf:
        copy.wait_recv()
    weight_step(0, z_2)
    last = []
    for i in range(3):
        w_f[i].wait_recv()
        block = w_rows(z_2, i)
        last.append(start(block, block, wl_s.at[i], wl_r.at[i], sibling))
    weight_step(1, z_p)
    zr0 = []
    gc[0].wait_recv()
    for i in range(3):
        rows, value = weight_join(z_2, i)
        g_part[z_2, c, rows] = value.astype(BF)
        zr0.append(z_reduce(0, i, z_2, z_m))
    for copy in last:
        copy.wait_recv()
    out_partial(z_2)
    out_start(z_2)
    yr0 = {d: y_copy(0, d) for d in ORDER}
    yr1 = {d: y_copy(1, d) for d in ORDER}
    started.extend(yr0.values())
    started.extend(yr1.values())
    transpose_weight(z_2)
    attended_partial(x_2)
    ar0 = start(a_part.at[x_2], a_recv.at[0], ar_s.at[0], ar_r.at[0], at_x(x_m))
    y_middle(2)
    weight_step(2, z_m)
    gc[1].wait_recv()
    zr1 = []
    for i in range(3):
        rows, value = weight_join(z_p, i)
        g_part[z_p, c, rows] = value.astype(BF)
        zr1.append(z_reduce(1, i, z_p, z_p))
    y_middle(1)
    attended_partial(x_p)
    ar1 = start(a_part.at[x_p], a_recv.at[1], ar_s.at[1], ar_r.at[1], at_x(x_p))
    y_middle(3)
    attended_partial(x_m)
    ar0.wait_recv()
    a_part[x_m] = (a_part[x_m].astype(F32) + a_recv[0].astype(F32)).astype(BF)
    ar2 = start(a_part.at[x_m], a_recv.at[2], ar_s.at[2], ar_r.at[2], at_x(x_m))
    y_middle(0)
    gc[2].wait_recv()
    zr2 = []
    for i in range(3):
        zr0[i].wait_recv()
        rows, value = weight_join(z_m, i)
        g_part[z_m, c, rows] = (value + g_recv[0, rows].astype(F32)).astype(BF)
        zr2.append(z_reduce(2, i, z_m, z_m))
    weight_step(3, zh)
    attended_partial(x)

    def out_final(j):
        value = o_part[y, j].astype(F32) + o_recv[1, j].astype(F32) + o_recv[2, j].astype(F32)
        return value.astype(BF)

    xo = []

    def out_send(d):
        to = (x + d) % 4
        yr1[d].wait_recv()
        yr2[d].wait_recv()
        o_part[y, to] = out_final(to)
        xo.append(start(o_part.at[y, to], rx.at[x], xo_s.at[d - 1], xo_r.at[d - 1], at_x(to)))

    gkv_acc[...] = jnp.zeros_like(gkv_acc)

    def backward_head(h, carry):
        rows = pl.ds(pl.multiple_of(h * HD, HD), HD)
        grad = a_part[x, rows, :]
        soft = probs[h]
        grad_p = jnp.dot(kv[:, HD:], grad, preferred_element_type=F32)
        dot = jnp.sum(soft * grad_p, axis=0, keepdims=True)
        grad_s = (soft * (grad_p - dot) * scale).astype(BF)
        gq_o[rows, :] = jnp.dot(kv_t[:HD, :], grad_s, preferred_element_type=F32).astype(BF)
        last = (((1,), (1,)), ((), ()))
        gkv_acc[:HD, :] += lax.dot_general(q_t[rows, :], grad_s, last, preferred_element_type=F32)
        gkv_acc[HD:, :] += lax.dot_general(grad, soft.astype(BF), last, preferred_element_type=F32)
        return carry

    def backward(first, past):
        lax.fori_loop(first, past, backward_head, 0)

    out_send(2)
    ar1.wait_recv()
    ar2.wait_recv()
    a_part[x] = (
        a_part[x].astype(F32) + a_recv[1].astype(F32) + a_recv[2].astype(F32)
    ).astype(BF)
    backward(0, 4)
    out_send(1)
    out_send(3)
    backward(4, 8)
    yr1[0].wait_recv()
    yr2[0].wait_recv()
    rx[x] = out_final(x)

    def zo_send(src):
        h = src % 2
        copy = send(rx.at[src], rz.at[h], zo_s.at[h], zo_r.at[h], partner)

        @pl.when(src // 2 != zl)
        def _():
            copy.start()

    zo_send(x)
    for copy, d in zip(xo, (2, 1, 3)):
        copy.wait_recv()
        zo_send((x + 4 - d) % 4)
    backward(8, HEADS)
    gkv_o[...] = jnp.transpose(gkv_acc[...]).astype(BF)
    gc[3].wait_recv()
    for i in range(3):
        zr1[i].wait_recv()
        zr2[i].wait_recv()
        rows, value = weight_join(zh, i)
        value += g_recv[1, rows].astype(F32) + g_recv[2, rows].astype(F32)
        if i < 2:
            gw_o[rows] = value.astype(BF)
        else:
            gw_o[pl.ds(2 * CHUNK, ROWS - 2 * CHUNK)] = value[: ROWS - 2 * CHUNK].astype(BF)

    for h in range(2):
        copy = send(rx.at[2 * (1 - zl) + h], rz.at[h], zo_s.at[h], zo_r.at[h], partner)
        copy.wait_recv()
        copy.wait_send()
    value = [
        (rx[2 * zl + q // 2, q % 2].astype(F32) + rz[q // 2, q % 2].astype(F32))[:ROWS]
        for q in range(4)
    ]
    out_o[...] = jnp.concatenate(value, axis=0).astype(BF)
    for copy in started:
        copy.wait_send()


def body(queries, keys_values, out_weight, cotangent):
    vmem = pl.BlockSpec(memory_space=pltpu.VMEM)
    dma = lambda *shape: pltpu.SemaphoreType.DMA(shape)
    scratch = [
        pltpu.VMEM((2 * HD, TOK), BF),
        pltpu.VMEM((2, 2, 2, PAD, TOK), BF),
        pltpu.VMEM((4, 4, 2, PAD, TOK), BF),
        pltpu.VMEM((4, 2, PAD, HCOL), BF),
        pltpu.VMEM((4, HCOL, TOK), BF),
        pltpu.VMEM((HEADS, TOK, TOK), F32),
        pltpu.VMEM((4, HCOL, 2 * PAD), BF),
        pltpu.VMEM((4, 4, 2, PAD, TOK), BF),
        pltpu.VMEM((3, 4, 2, PAD, TOK), BF),
        pltpu.VMEM((4, 2, PAD, TOK), BF),
        pltpu.VMEM((2, 2, PAD, TOK), BF),
        pltpu.VMEM((4, 2, PAD, HCOL), BF),
        pltpu.VMEM((4, PAD, HCOL), BF),
        pltpu.VMEM((3, PAD, HCOL), BF),
        pltpu.VMEM((4, HCOL, TOK), BF),
        pltpu.VMEM((3, HCOL, TOK), BF),
        pltpu.VMEM((2 * HD, TOK), F32),
        dma(3), dma(3), dma(2), dma(2), dma(2, 3), dma(2, 3), dma(3, 2, 4), dma(3, 2, 4), dma(3, 3), dma(3, 3), dma(4), dma(4),
        dma(3, 3), dma(3, 3), dma(3, 4), dma(3, 4), dma(3), dma(3), dma(2), dma(2),
        dma(4), dma(4), dma(3, 3), dma(3, 3), dma(3), dma(3),
    ]
    out, gq, gkv, gw = pl.pallas_call(
        kernel,
        out_shape=(
            jax.ShapeDtypeStruct((4 * ROWS, TOK), BF),
            jax.ShapeDtypeStruct((HCOL, TOK), BF),
            jax.ShapeDtypeStruct((TOK, 2 * HD), BF),
            jax.ShapeDtypeStruct((ROWS, HCOL), BF),
        ),
        in_specs=[vmem] * 4,
        out_specs=(vmem,) * 4,
        scratch_shapes=scratch,
        compiler_params=pltpu.CompilerParams(
            collective_id=0, has_side_effects=True, vmem_limit_bytes=60 * 2**20
        ),
        cost_estimate=pl.CostEstimate(flops=12 * 10**9, bytes_accessed=5 * 10**6, transcendentals=10**6),
    )(queries.T, keys_values, out_weight, cotangent.T)
    return out.T, gq.T, gkv, gw


def solution(mesh):
    spec = P("dp", "tensor")
    return jax.shard_map(
        body, mesh=mesh, in_specs=(spec,) * 4, out_specs=(spec,) * 4, check_vma=False
    )
```
